512 devices in a mesh: front: 16 (over y, x), tile: 32 (over z, core).
Axes of the slice: x: 4, y: 4, z: 16, core: 2. Of those that a mesh axis runs over, the one named last changes fastest.
Arguments:
- pool: bfloat16 [16, 32768, 256], P('front', 'tile'), may hold values from -6 to 6
- nbr_owner: int32 [16, 256, 1024, 1], P('front', 'tile'), may hold values from 0 to 31; in each aligned block of 8192 rows (0 to 8191, 8192 to 16383, ..., all dimensions but the last counted through in order) at most 512 rows name the same one
- nbr_row: int32 [16, 256, 1024], P('front', 'tile'), may hold values from 0 to 1023
- nbr_count: int32 [16, 256], P('front', 'tile'), may hold values from 512 to 1024
- normal_draw: bfloat16 [16, 256, 256, 256], P('front', 'tile'), may hold values from -6 to 6
- kriging_weight: bfloat16 [256, 1024], replicated, may hold values from -0.1875 to 0.1875
- noise_factor: bfloat16 [256, 256], replicated, may hold values from -0.375 to 0.375
- face_weight: float32 [256, 32], replicated, may hold values from -1 to 1
Outputs:
- evolved: bfloat16 [16, 256, 256, 256], P('front', 'tile')
The draws below stay inside these ranges and needn't reach their ends.
Inputs may be any that keep to these rules, and one draw needn't show every extreme that they name: `nbr_owner`: among the entries of one device's blocks, no owner is named by more than 512 entries, a bound that some block reaches.
All inputs are finite; a program needn't handle non-finite values.
Results may differ from the reference program's by a relative error of at most 0.0013.
Values may be sent and summed in bfloat16 or wider, within the bound.
No kernel may reach another device: no remote copies, remote signals or barrier semaphores. Data moves between devices by JAX's collectives and lax.ppermute only.
A program may use at most 64 MiB of HBM per device.

```python
import math
import jax
import jax.numpy as jnp
import numpy as np
from jax import lax

R = 256
BLK = 256
NBR = 1024
EDGE = 32
BLOCKS_DEV = 8
POOL_DEV = 1024
CAP = 512
NBLOCKS = 256
POOL = 32768
N_FRONT = 16
N_TILE = 32


def place_ends(values, key, smallest, high):
    dims = values.shape
    index_at = [jax.random.randint(jax.random.fold_in(key, axis), (), 0, dims[axis]) for axis in range(len(dims))]
    values = values.at[tuple(index_at)].set(smallest)
    longest = dims.index(max(dims))
    index_at[longest] = (index_at[longest] + 1) % dims[longest]
    return values.at[tuple(index_at)].set(high)


def shard_levels(stream_key, shape, shards, least, high):
    gain, own = 1.0, jax.random.fold_in(stream_key, 6)
    for position, shards_of in shards:
        steps = jnp.exp(jax.random.uniform(jax.random.fold_in(own, position), (shards_of,), jnp.float32, least / len(shards), high / len(shards)))
        gain = gain * jnp.repeat(steps, shape[position] // shards_of).reshape([-1 if axis == position else 1 for axis in range(len(shape))])
    return gain


def routed_block(rng, own, number, rows, amount, top, reach, lean):
    ranking = jax.random.permutation(rng, amount)
    crowded, usual = portions_of(amount, rows * top, reach, lean, True), portions_of(amount, rows * top, reach, lean, False)
    places = jnp.arange(amount)

    def named(sizes, rotation):
        used = int((sizes > 0).sum())
        fixed = max(1, used // 4)
        moved = fixed + (places - fixed + rotation * (used - fixed)) % max(1, amount - fixed)
        return jnp.zeros((amount,), jnp.int32).at[ranking[jnp.where(places < fixed, places, moved)]].set(jnp.asarray(sizes, jnp.int32))

    sizes = jnp.where(number % 4 == 0, named(crowded, number // 4), named(usual, number - number // 4 - 1))
    mixed = jax.random.permutation(jax.random.fold_in(own, 3), amount)
    giver, taker = mixed[0:amount // 2 * 2:2], mixed[1:amount // 2 * 2:2]
    margin = jnp.minimum(sizes[giver] - 1, reach - sizes[taker]) // 2
    margin = jnp.where((giver == ranking[0]) | (taker == ranking[0]) | (sizes[taker] == 0), 0, jnp.maximum(margin, 0))
    moved = jax.random.randint(jax.random.fold_in(own, 4), (amount // 2,), 0, 1 << 20) % (margin + 1)
    sizes = sizes.at[giver].add(-moved).at[taker].add(moved)
    items = jnp.searchsorted(jnp.cumsum(sizes), jnp.arange(rows * top), side="right").astype(jnp.int32)
    table = items.reshape(top, rows).T
    table = table[jax.random.permutation(jax.random.fold_in(own, 1), rows)]
    rotation = jax.random.randint(jax.random.fold_in(own, 2), (rows, 1), 0, top)
    return jnp.take_along_axis(table, (jnp.arange(top)[None, :] + rotation) % top, axis=1)


def portions_of(amount, total, bound, skew, full):
    weights = [(1 << 20) // math.isqrt(standing ** skew) + 1 for standing in range(1, amount + 1)]
    largest = bound if full else min(bound, max(-(-total // amount), total * weights[0] // sum(weights)))
    least = 1 if total - largest >= amount - 1 else 0
    holding, spare = [largest] + [least] * (amount - 1), total - largest - least * (amount - 1)
    while spare > 0:
        candidates = [i for i in range(1, amount) if holding[i] < largest] or [i for i in range(1, amount) if holding[i] < bound]
        mass, budget = sum([weights[i] for i in candidates]), spare
        for i in candidates:
            extra = min(bound - holding[i], max(1, budget * weights[i] // mass), spare)
            holding[i] = holding[i] + extra
            spare = spare - extra
    return np.array(holding)


def centred(own_key, extent, deviation, reach, cuts=(), kind=jnp.bfloat16):
    loudness = shard_levels(own_key, extent, cuts, -0.22, 0.18) if cuts else 1.0
    drawn = jax.random.normal(own_key, extent, jnp.float32) * deviation * loudness
    return jnp.minimum(jnp.maximum(drawn, -reach), reach).astype(kind)


def setup_inputs(seed: int = 0) -> dict:
    arg_keys = jax.random.split(jax.random.key(seed), 9)
    pool = centred(arg_keys[0], (N_FRONT, POOL, R), 1.0, 6.0, ((0, 16), (1, 32)))
    nbr_owner_keys = jax.random.split(jax.random.fold_in(arg_keys[1], 1), N_FRONT * NBLOCKS * NBR // (BLOCKS_DEV * NBR))
    nbr_owner_turns = jax.random.permutation(jax.random.fold_in(arg_keys[1], 3), N_FRONT * NBLOCKS * NBR // (BLOCKS_DEV * NBR))
    nbr_owner = jax.vmap(lambda own, number: routed_block(jax.random.fold_in(arg_keys[1], 2), own, number, BLOCKS_DEV * NBR, N_TILE, 1, CAP, 2))(nbr_owner_keys, nbr_owner_turns).reshape((N_FRONT, NBLOCKS, NBR, 1))
    nbr_row = place_ends(jax.random.randint(arg_keys[2], (N_FRONT, NBLOCKS, NBR), 0, POOL_DEV), jax.random.fold_in(arg_keys[2], 1), 0, POOL_DEV - 1).astype(jnp.int32)
    nbr_count = place_ends(jax.random.randint(arg_keys[3], (N_FRONT, NBLOCKS), NBR // 2, NBR + 1), jax.random.fold_in(arg_keys[3], 1), NBR // 2, NBR).astype(jnp.int32)
    normal_draw = centred(arg_keys[4], (N_FRONT, NBLOCKS, BLK, R), 1.0, 6.0, ((0, 16), (1, 32)))
    kriging_weight = centred(arg_keys[5], (BLK, NBR), NBR ** -0.5, 0.1875)
    noise_factor = centred(arg_keys[6], (BLK, BLK), BLK ** -0.5, 0.375)
    face_weight = centred(arg_keys[7], (BLK, EDGE), (EDGE + EDGE // 4) ** -0.5, 1.0, (), jnp.float32)
    return dict(pool=pool, nbr_owner=nbr_owner, nbr_row=nbr_row, nbr_count=nbr_count, normal_draw=normal_draw, kriging_weight=kriging_weight, noise_factor=noise_factor, face_weight=face_weight)


def reference(pool, nbr_owner, nbr_row, nbr_count, normal_draw, kriging_weight, noise_factor, face_weight):
    lower_factor = jnp.tril(noise_factor).astype(jnp.float32)
    kriging = kriging_weight.astype(jnp.float32)
    outputs = []
    below = jnp.zeros((NBLOCKS, EDGE, R), jnp.float32)
    for front_row in range(N_FRONT):
        pool_index = (nbr_owner[front_row, :, :, 0] * POOL_DEV + nbr_row[front_row]).astype(jnp.int32)
        values = jnp.take(pool[front_row], pool_index, axis=0)
        is_live = jnp.arange(NBR)[None, :] < nbr_count[front_row][:, None]
        values = jnp.where(is_live[:, :, None], values, jnp.zeros((), values.dtype))
        local_part = jnp.einsum("cn,bnr->bcr", kriging, values.astype(jnp.float32))
        local_part = local_part + jnp.einsum("cd,bdr->bcr", lower_factor, normal_draw[front_row].astype(jnp.float32))
        state = local_part + jnp.einsum("ce,ber->bcr", face_weight, below, precision=lax.Precision.HIGHEST)
        below = state[:, BLK - EDGE:, :]
        outputs.append(state.astype(jnp.bfloat16))
    return jnp.stack(outputs, axis=0)
```

```python
import functools

import jax
import jax.numpy as jnp
from jax import lax
from jax.experimental import pallas as pl
from jax.experimental.pallas import tpu as pltpu
from jax.sharding import PartitionSpec as P

LANES = 128
UNROLL = 16
PIECES = 8
HIGHEST = lax.Precision.HIGHEST


def gather_kernel(
    pair_ref, count_ref, pool_hbm, live_ref, weight_ref, noise_ref, draw_ref,
    local_ref, edge_ref, pool, values, sems,
):
    blocks, entries = pair_ref.shape
    halves, edge = pool.shape[1], edge_ref.shape[1]
    cells = weight_ref.shape[0]
    rows = pool.shape[0] // PIECES
    copies = [
        pltpu.make_async_copy(
            pool_hbm.at[pl.ds(i * rows, rows)], pool.at[pl.ds(i * rows, rows)], sems.at[i]
        )
        for i in range(PIECES)
    ]
    for copy in copies:
        copy.start()
    values[...] = jnp.zeros_like(values)
    for b in range(blocks):
        local_ref[b] = jnp.dot(
            noise_ref[...], draw_ref[b], preferred_element_type=jnp.float32
        )
    for copy in copies:
        copy.wait()

    def block(b, _):
        def some(i, _):
            base = pl.multiple_of(i * UNROLL, UNROLL)
            places = [pair_ref[b, base + u] for u in range(UNROLL)]
            found = [[pool[p, h] for p in places] for h in range(halves)]
            for h in range(halves):
                for u in range(UNROLL):
                    values[h, base + u] = found[h][u]
            return 0

        lax.fori_loop(0, (count_ref[b] + UNROLL - 1) // UNROLL, some, 0)
        listed = jnp.concatenate(
            [values.at[h].reshape(2 * entries, LANES)[...] for h in range(halves)], axis=1
        )
        total = local_ref[b] + jnp.dot(
            weight_ref[...] * live_ref[b], listed, preferred_element_type=jnp.float32
        )
        local_ref[b] = total
        for h in range(halves):
            edge_ref[halves * b + h] = total[cells - edge :, h * LANES : (h + 1) * LANES]
        return 0

    lax.fori_loop(0, blocks, block, 0)


def gather_call(pair, count, pool, live, weight2, lower, draw, edge):
    blocks, entries = pair.shape
    cells, realizations = draw.shape[1:]
    halves = pool.shape[1]
    smem = pl.BlockSpec(memory_space=pltpu.SMEM)
    vmem = pl.BlockSpec(memory_space=pltpu.VMEM)
    return pl.pallas_call(
        gather_kernel,
        out_shape=(
            jax.ShapeDtypeStruct((blocks, cells, realizations), jnp.float32),
            jax.ShapeDtypeStruct((blocks * halves, edge, LANES), jnp.float32),
        ),
        in_specs=[smem, smem, pl.BlockSpec(memory_space=pl.ANY), vmem, vmem, vmem, vmem],
        out_specs=(vmem, vmem),
        scratch_shapes=[
            pltpu.VMEM(pool.shape, pool.dtype),
            pltpu.VMEM((halves, entries, 2, LANES), pool.dtype),
            pltpu.SemaphoreType.DMA((PIECES,)),
        ],
        compiler_params=pltpu.CompilerParams(vmem_limit_bytes=50 * 2**20),
        cost_estimate=pl.CostEstimate(
            flops=2 * blocks * cells * (2 * entries + cells) * realizations,
            bytes_accessed=5 * 2**24,
            transcendentals=0,
        ),
        name="gather",
    )(pair, count, pool, live, weight2, lower, draw)


def scan_kernel(scan_ref, face_ref, out_ref):
    out_ref[...] = jnp.dot(
        scan_ref[...], face_ref[...], precision=HIGHEST, preferred_element_type=jnp.float32
    )


def scan_call(scan, face):
    return pl.pallas_call(
        scan_kernel,
        out_shape=jax.ShapeDtypeStruct(face.shape, face.dtype),
        compiler_params=pltpu.CompilerParams(vmem_limit_bytes=16 * 2**20),
        name="scan",
    )(scan, face)


def finish_kernel(local_ref, face_ref, below_ref, out_ref):
    halves = local_ref.shape[2] // LANES
    for b in range(local_ref.shape[0]):
        below = jnp.concatenate([below_ref[halves * b + h] for h in range(halves)], axis=1)
        state = local_ref[b] + jnp.dot(
            face_ref[...], below, precision=HIGHEST, preferred_element_type=jnp.float32
        )
        out_ref[b] = state.astype(out_ref.dtype)


def finish_call(local, face, below):
    return pl.pallas_call(
        finish_kernel,
        out_shape=jax.ShapeDtypeStruct(local.shape, jnp.bfloat16),
        compiler_params=pltpu.CompilerParams(vmem_limit_bytes=16 * 2**20),
        name="finish",
    )(local, face, below)


def scan_matrix(square, count):
    edge = square.shape[0]
    mm = functools.partial(jnp.dot, precision=HIGHEST)
    powers = jnp.concatenate([square, jnp.eye(edge, dtype=square.dtype)], axis=1)
    top = mm(square, square)
    while powers.shape[1] < count * edge:
        powers = jnp.concatenate([mm(top, powers), powers], axis=1)
        top = mm(top, top)
    powers = powers[:, -(count - 1) * edge :]
    strip = jnp.concatenate([powers, jnp.zeros((edge, count * edge), powers.dtype)], axis=1)
    starts = [(count - 1 - f) * edge for f in range(count)]
    return jnp.concatenate([strip[:, s : s + count * edge] for s in starts])


def body(
    pool, nbr_owner, nbr_row, nbr_count, normal_draw, kriging_weight, noise_factor, face_weight
):
    pool_rows, realizations = pool.shape[1:]
    entries = nbr_row.shape[2]
    edge = face_weight.shape[1]
    halves = realizations // LANES
    front_count = lax.axis_size("front")
    mine = pool[0].reshape(pool_rows // 2, 2, halves, LANES).transpose(0, 2, 1, 3)
    gathered = lax.all_gather(mine, "tile", tiled=True)
    index = nbr_owner[0, :, :, 0] * pool_rows + nbr_row[0]
    pair = index >> 1
    count = nbr_count[0]
    is_live = jnp.arange(entries)[None, :] < count[:, None]
    live = (index & 1)[:, :, None] == jnp.arange(2)[None, None, :]
    live = (live & is_live[:, :, None]).astype(jnp.bfloat16).reshape(-1, 1, 2 * entries)
    weight2 = jnp.repeat(kriging_weight, 2, axis=1)
    scan = scan_matrix(face_weight[-edge:], front_count)
    local, face = gather_call(
        pair, count, gathered, live, weight2, jnp.tril(noise_factor), normal_draw[0], edge
    )
    swap = functools.partial(
        lax.all_to_all, axis_name="front", split_axis=0, concat_axis=0, tiled=True
    )
    below = scan_call(scan, swap(face).reshape(-1, LANES)).reshape(face.shape)
    return finish_call(local, face_weight, swap(below))[None]


def solution(mesh):
    placed = (
        P("front", "tile", None),
        P("front", "tile", None, None),
        P("front", "tile", None),
        P("front", "tile"),
        P("front", "tile", None, None),
        P(),
        P(),
        P(),
    )
    return jax.shard_map(
        body, mesh=mesh, in_specs=placed, out_specs=P("front", "tile", None, None), check_vma=False
    )
```

```python
import functools

import jax
import jax.numpy as jnp
from jax import lax
from jax.experimental import pallas as pl
from jax.experimental.pallas import tpu as pltpu
from jax.sharding import PartitionSpec as P

LANES = 128
UNROLL = 32
PIECES = 8
PAIRS = 4
HIGHEST = lax.Precision.HIGHEST


def gather_kernel(
    tile_ref, count_ref, pool_hbm, live_ref, weight_ref, noise_ref, draw_ref,
    local_ref, edge_ref, pool, values, sems,
):
    blocks, cells, realizations = local_ref.shape
    halves, entries = values.shape[:2]
    edge = edge_ref.shape[1]
    rows = pool.shape[0] // PIECES
    copies = [
        pltpu.make_async_copy(
            pool_hbm.at[pl.ds(i * rows, rows)], pool.at[pl.ds(i * rows, rows)], sems.at[i]
        )
        for i in range(PIECES)
    ]
    for copy in copies:
        copy.start()
    values[...] = jnp.zeros_like(values)
    for b in range(blocks):
        local_ref[b] = jnp.dot(
            noise_ref[...], draw_ref[b], preferred_element_type=jnp.float32
        )
    for copy in copies:
        copy.wait()

    def block(b, _):
        def some(i, _):
            base = pl.multiple_of(i * UNROLL, UNROLL)
            places = [tile_ref[b * entries + base + u] for u in range(UNROLL)]
            found = [[pool[p + h * PAIRS] for p in places] for h in range(halves)]
            for h in range(halves):
                for u in range(UNROLL):
                    values[h, base + u] = found[h][u]
            return 0

        lax.fori_loop(0, (count_ref[b] + UNROLL - 1) // UNROLL, some, 0)
        listed = jnp.concatenate(
            [values.at[h].reshape(2 * entries, LANES)[...] for h in range(halves)], axis=1
        )
        total = local_ref[b] + jnp.dot(
            weight_ref[...] * live_ref[b], listed, preferred_element_type=jnp.float32
        )
        local_ref[b] = total
        for h in range(halves):
            edge_ref[halves * b + h] = total[cells - edge :, h * LANES : (h + 1) * LANES]
        return 0

    lax.fori_loop(0, blocks, block, 0)


def gather_call(tile, count, pool, live, weight2, lower, draw, edge):
    blocks, cells, realizations = draw.shape
    halves = realizations // LANES
    entries = tile.shape[0] // blocks
    smem = pl.BlockSpec(memory_space=pltpu.SMEM)
    vmem = pl.BlockSpec(memory_space=pltpu.VMEM)
    return pl.pallas_call(
        gather_kernel,
        out_shape=(
            jax.ShapeDtypeStruct((blocks, cells, realizations), jnp.float32),
            jax.ShapeDtypeStruct((blocks * halves, edge, LANES), jnp.float32),
        ),
        in_specs=[smem, smem, pl.BlockSpec(memory_space=pl.ANY), vmem, vmem, vmem, vmem],
        out_specs=(vmem, vmem),
        scratch_shapes=[
            pltpu.VMEM(pool.shape, pool.dtype),
            pltpu.VMEM((halves, entries, 2, LANES), pool.dtype),
            pltpu.SemaphoreType.DMA((PIECES,)),
        ],
        compiler_params=pltpu.CompilerParams(vmem_limit_bytes=50 * 2**20),
        cost_estimate=pl.CostEstimate(
            flops=2 * blocks * cells * (2 * entries + cells) * realizations,
            bytes_accessed=5 * 2**24,
            transcendentals=0,
        ),
        name="gather",
    )(tile, count, pool, live, weight2, lower, draw)


def scan_kernel(scan_ref, face_ref, out_ref):
    out_ref[...] = jnp.dot(
        scan_ref[...], face_ref[...], precision=HIGHEST, preferred_element_type=jnp.float32
    )


def scan_call(scan, face):
    return pl.pallas_call(
        scan_kernel,
        out_shape=jax.ShapeDtypeStruct(face.shape, face.dtype),
        compiler_params=pltpu.CompilerParams(vmem_limit_bytes=16 * 2**20),
        name="scan",
    )(scan, face)


def finish_kernel(local_ref, face_ref, below_ref, out_ref):
    halves = below_ref.shape[0]
    below = jnp.concatenate([below_ref[h] for h in range(halves)], axis=1)
    state = local_ref[0] + jnp.dot(
        face_ref[...], below, precision=HIGHEST, preferred_element_type=jnp.float32
    )
    out_ref[0] = state.astype(out_ref.dtype)


def finish_call(local, face, below):
    blocks, cells, realizations = local.shape
    edge = face.shape[1]
    halves = realizations // LANES
    whole = pl.BlockSpec((1, cells, realizations), lambda b: (b, 0, 0))
    return pl.pallas_call(
        finish_kernel,
        grid=(blocks,),
        out_shape=jax.ShapeDtypeStruct(local.shape, jnp.bfloat16),
        in_specs=[
            whole,
            pl.BlockSpec((cells, edge), lambda b: (0, 0)),
            pl.BlockSpec((halves, edge, LANES), lambda b: (b, 0, 0)),
        ],
        out_specs=whole,
        name="finish",
    )(local, face, below)


def scan_matrix(square, count):
    edge = square.shape[0]
    mm = functools.partial(jnp.dot, precision=HIGHEST)
    powers = jnp.concatenate([square, jnp.eye(edge, dtype=square.dtype)], axis=1)
    top = mm(square, square)
    while powers.shape[1] < count * edge:
        powers = jnp.concatenate([mm(top, powers), powers], axis=1)
        top = mm(top, top)
    powers = powers[:, -(count - 1) * edge :]
    strip = jnp.concatenate([powers, jnp.zeros((edge, count * edge), powers.dtype)], axis=1)
    starts = [(count - 1 - f) * edge for f in range(count)]
    return jnp.concatenate([strip[:, s : s + count * edge] for s in starts])


def body(
    pool, nbr_owner, nbr_row, nbr_count, normal_draw, kriging_weight, noise_factor, face_weight
):
    pool_rows, realizations = pool.shape[1:]
    entries = nbr_row.shape[2]
    edge = face_weight.shape[1]
    halves = realizations // LANES
    front_count = lax.axis_size("front")
    group = 2 * PAIRS
    gathered = lax.all_gather(pool[0], "tile", tiled=True)
    pieces = gathered.reshape(-1, PAIRS, 2, halves, LANES).transpose(0, 3, 1, 2, 4)
    pieces = pieces.reshape(-1, 2, LANES)
    index = nbr_owner[0, :, :, 0] * pool_rows + nbr_row[0]
    tile = index // group * (halves * PAIRS) + index % group // 2
    count = nbr_count[0]
    is_live = jnp.arange(entries)[None, :] < count[:, None]
    live = (index & 1)[:, :, None] == jnp.arange(2)[None, None, :]
    live = (live & is_live[:, :, None]).astype(jnp.bfloat16).reshape(-1, 1, 2 * entries)
    weight2 = jnp.repeat(kriging_weight, 2, axis=1)
    scan = scan_matrix(face_weight[-edge:], front_count)
    local, face = gather_call(
        tile.reshape(-1), count, pieces, live, weight2, jnp.tril(noise_factor), normal_draw[0], edge
    )
    swap = functools.partial(
        lax.all_to_all, axis_name="front", split_axis=0, concat_axis=0, tiled=True
    )
    below = scan_call(scan, swap(face).reshape(-1, LANES)).reshape(face.shape)
    return finish_call(local, face_weight, swap(below))[None]


def solution(mesh):
    placed = (
        P("front", "tile", None),
        P("front", "tile", None, None),
        P("front", "tile", None),
        P("front", "tile"),
        P("front", "tile", None, None),
        P(),
        P(),
        P(),
    )
    return jax.shard_map(
        body, mesh=mesh, in_specs=placed, out_specs=P("front", "tile", None, None), check_vma=False
    )
```

```python
import functools

import jax
import jax.numpy as jnp
from jax import lax
from jax.experimental import pallas as pl
from jax.experimental.pallas import tpu as pltpu
from jax.sharding import PartitionSpec as P

LANES = 128
UNROLL = 32
PIECES = 8
PAIRS = 4
REST = 320
SCALE = 2.0**13
FINISH_BLOCKS = 4
HIGHEST = lax.Precision.HIGHEST


def gather_kernel(
    tile_ref, count_ref, main_hbm, rest_hbm, live_ref, weight_ref, noise_ref, draw_ref,
    local_ref, edge_ref, pool, values, sems,
):
    blocks, cells, realizations = local_ref.shape
    halves, entries = values.shape[:2]
    edge = edge_ref.shape[1]
    copies, start = [], 0
    for source in (rest_hbm, main_hbm):
        rows = source.shape[0] // PIECES
        for i in range(PIECES):
            copies.append(
                pltpu.make_async_copy(
                    source.at[pl.ds(i * rows, rows)],
                    pool.at[pl.ds(start + i * rows, rows)],
                    sems.at[len(copies)],
                )
            )
        start += source.shape[0]
    for copy in copies:
        copy.start()
    values[...] = jnp.zeros_like(values)
    for b in range(blocks):
        local_ref[b] = jnp.dot(
            noise_ref[...], draw_ref[b], preferred_element_type=jnp.float32
        )
    for copy in copies:
        copy.wait()

    def block(b, _):
        def some(i, _):
            base = pl.multiple_of(i * UNROLL, UNROLL)
            places = [tile_ref[b * entries + base + u] for u in range(UNROLL)]
            found = [[pool[p + h * PAIRS] for p in places] for h in range(halves)]
            for h in range(halves):
                for u in range(UNROLL):
                    values[h, base + u] = found[h][u]
            return 0

        lax.fori_loop(0, (count_ref[b] + UNROLL - 1) // UNROLL, some, 0)
        listed = jnp.concatenate(
            [values.at[h].reshape(2 * entries, LANES)[...] for h in range(halves)], axis=1
        )
        total = local_ref[b] + jnp.dot(
            weight_ref[...] * live_ref[b], listed, preferred_element_type=jnp.float32
        )
        local_ref[b] = total
        for h in range(halves):
            edge_ref[halves * b + h] = total[cells - edge :, h * LANES : (h + 1) * LANES]
        return 0

    lax.fori_loop(0, blocks, block, 0)


def gather_call(tile, count, main, rest, live, weight2, lower, draw, edge):
    blocks, cells, realizations = draw.shape
    halves = realizations // LANES
    entries = tile.shape[0] // blocks
    smem = pl.BlockSpec(memory_space=pltpu.SMEM)
    vmem = pl.BlockSpec(memory_space=pltpu.VMEM)
    hbm = pl.BlockSpec(memory_space=pl.ANY)
    return pl.pallas_call(
        gather_kernel,
        out_shape=(
            jax.ShapeDtypeStruct((blocks, cells, realizations), jnp.float32),
            jax.ShapeDtypeStruct((blocks * halves, edge, LANES), jnp.float32),
        ),
        in_specs=[smem, smem, hbm, hbm, vmem, vmem, vmem, vmem],
        out_specs=(vmem, vmem),
        scratch_shapes=[
            pltpu.VMEM((main.shape[0] + rest.shape[0], 2, LANES), main.dtype),
            pltpu.VMEM((halves, entries, 2, LANES), main.dtype),
            pltpu.SemaphoreType.DMA((2 * PIECES,)),
        ],
        compiler_params=pltpu.CompilerParams(vmem_limit_bytes=50 * 2**20),
        cost_estimate=pl.CostEstimate(
            flops=2 * blocks * cells * (2 * entries + cells) * realizations,
            bytes_accessed=5 * 2**24,
            transcendentals=0,
        ),
        name="gather",
    )(tile, count, main, rest, live, weight2, lower, draw)


def scan_kernel(scan_ref, face_ref, out_ref):
    out_ref[...] = jnp.dot(
        scan_ref[...], face_ref[...], precision=HIGHEST, preferred_element_type=jnp.float32
    )


def scan_call(scan, face):
    return pl.pallas_call(
        scan_kernel,
        out_shape=jax.ShapeDtypeStruct(face.shape, face.dtype),
        compiler_params=pltpu.CompilerParams(vmem_limit_bytes=16 * 2**20),
        name="scan",
    )(scan, face)


def finish_kernel(local_ref, face_ref, below_ref, out_ref):
    blocks, _, realizations = local_ref.shape
    halves = realizations // LANES
    for b in range(blocks):
        below = jnp.concatenate([below_ref[halves * b + h] for h in range(halves)], axis=1)
        state = local_ref[b] + jnp.dot(
            face_ref[...], below, precision=HIGHEST, preferred_element_type=jnp.float32
        )
        out_ref[b] = state.astype(out_ref.dtype)


def finish_call(local, face, below):
    blocks, cells, realizations = local.shape
    edge = face.shape[1]
    halves = realizations // LANES
    size = FINISH_BLOCKS
    whole = pl.BlockSpec((size, cells, realizations), lambda b: (b, 0, 0))
    return pl.pallas_call(
        finish_kernel,
        grid=(blocks // size,),
        out_shape=jax.ShapeDtypeStruct(local.shape, jnp.bfloat16),
        in_specs=[
            whole,
            pl.BlockSpec((cells, edge), lambda b: (0, 0)),
            pl.BlockSpec((size * halves, edge, LANES), lambda b: (b, 0, 0)),
        ],
        out_specs=whole,
        name="finish",
    )(local, face, below)


def scan_matrix(square, count):
    edge = square.shape[0]
    mm = functools.partial(jnp.dot, precision=HIGHEST)
    powers = jnp.concatenate([square, jnp.eye(edge, dtype=square.dtype)], axis=1)
    top = mm(square, square)
    while powers.shape[1] < count * edge:
        powers = jnp.concatenate([mm(top, powers), powers], axis=1)
        top = mm(top, top)
    powers = powers[:, -(count - 1) * edge :]
    strip = jnp.concatenate([powers, jnp.zeros((edge, count * edge), powers.dtype)], axis=1)
    starts = [(count - 1 - f) * edge for f in range(count)]
    return jnp.concatenate([strip[:, s : s + count * edge] for s in starts])


def body(
    pool, nbr_owner, nbr_row, nbr_count, normal_draw, kriging_weight, noise_factor, face_weight
):
    pool_rows, realizations = pool.shape[1:]
    entries = nbr_row.shape[2]
    edge = face_weight.shape[1]
    halves = realizations // LANES
    front_count = lax.axis_size("front")
    group = 2 * PAIRS
    tiles = lax.axis_size("tile")

    def as_pieces(rows):
        rows = rows.reshape(-1, PAIRS, 2, halves, LANES).transpose(0, 3, 1, 2, 4)
        return rows.reshape(-1, 2, LANES)

    main_rows = pool_rows - REST
    main = as_pieces(lax.all_gather(pool[0, :main_rows], "tile", tiled=True))
    scaled = (pool[0, main_rows:] * SCALE).astype(jnp.float16)
    rest = lax.all_gather(scaled, "tile", tiled=True)
    rest = as_pieces(rest.astype(pool.dtype) * jnp.asarray(1 / SCALE, pool.dtype))
    owner, row = nbr_owner[0, :, :, 0], nbr_row[0]
    index = jnp.where(
        row < main_rows,
        tiles * REST + owner * main_rows + row,
        owner * REST + row - main_rows,
    )
    tile = index // group * (halves * PAIRS) + index % group // 2
    count = nbr_count[0]
    is_live = jnp.arange(entries)[None, :] < count[:, None]
    live = (index & 1)[:, :, None] == jnp.arange(2)[None, None, :]
    live = (live & is_live[:, :, None]).astype(jnp.bfloat16).reshape(-1, 1, 2 * entries)
    weight2 = jnp.repeat(kriging_weight, 2, axis=1)
    scan = scan_matrix(face_weight[-edge:], front_count)
    local, face = gather_call(
        tile.reshape(-1), count, main, rest, live, weight2, jnp.tril(noise_factor), normal_draw[0], edge
    )
    swap = functools.partial(
        lax.all_to_all, axis_name="front", split_axis=0, concat_axis=0, tiled=True
    )
    below = scan_call(scan, swap(face).reshape(-1, LANES)).reshape(face.shape)
    return finish_call(local, face_weight, swap(below))[None]


def solution(mesh):
    placed = (
        P("front", "tile", None),
        P("front", "tile", None, None),
        P("front", "tile", None),
        P("front", "tile"),
        P("front", "tile", None, None),
        P(),
        P(),
        P(),
    )
    return jax.shard_map(
        body, mesh=mesh, in_specs=placed, out_specs=P("front", "tile", None, None), check_vma=False
    )
```

```python
import functools

import jax
import jax.numpy as jnp
from jax import lax
from jax.experimental import pallas as pl
from jax.experimental.pallas import tpu as pltpu
from jax.sharding import PartitionSpec as P

LANES = 128
UNROLL = 32
PIECES = 16
PAIRS = 4
FINISH_BLOCKS = 4
HIGHEST = lax.Precision.HIGHEST


def gather_kernel(
    tile_ref, count_ref, pool_hbm, live_ref, weight_ref, noise_ref, draw_ref,
    local_hbm, edge_ref, pool, values, local_ref, sems, local_sems,
):
    blocks, cells, _ = local_ref.shape
    halves, entries = values.shape[:2]
    edge = edge_ref.shape[1]
    rows = pool.shape[0] // PIECES
    copies = [
        pltpu.make_async_copy(
            pool_hbm.at[pl.ds(i * rows, rows)], pool.at[pl.ds(i * rows, rows)], sems.at[i]
        )
        for i in range(PIECES)
    ]
    for i, copy in enumerate(copies):
        copy.start(priority=i % 2)
    values[...] = jnp.zeros_like(values)
    for b in range(blocks):
        local_ref[b] = jnp.dot(
            noise_ref[...], draw_ref[b], preferred_element_type=jnp.float32
        )
    for copy in copies:
        copy.wait()

    def keep(b):
        return pltpu.make_async_copy(local_ref.at[b], local_hbm.at[b], local_sems.at[b])

    def block(b, _):
        def some(i, _):
            base = pl.multiple_of(i * UNROLL, UNROLL)
            places = [tile_ref[b * entries + base + u] for u in range(UNROLL)]
            found = [[pool[p + h * PAIRS] for p in places] for h in range(halves)]
            for h in range(halves):
                for u in range(UNROLL):
                    values[h, base + u] = found[h][u]
            return 0

        lax.fori_loop(0, (count_ref[b] + UNROLL - 1) // UNROLL, some, 0)
        listed = jnp.concatenate(
            [values.at[h].reshape(2 * entries, LANES)[...] for h in range(halves)], axis=1
        )
        total = local_ref[b] + jnp.dot(
            weight_ref[...] * live_ref[b], listed, preferred_element_type=jnp.float32
        )
        local_ref[b] = total
        for h in range(halves):
            edge_ref[halves * b + h] = total[cells - edge :, h * LANES : (h + 1) * LANES]
        keep(b).start()
        return 0

    lax.fori_loop(0, blocks, block, 0)
    for b in range(blocks):
        keep(b).wait()


def gather_call(tile, count, pool, live, weight2, lower, draw, edge):
    blocks, cells, realizations = draw.shape
    halves = realizations // LANES
    entries = tile.shape[0] // blocks
    smem = pl.BlockSpec(memory_space=pltpu.SMEM)
    vmem = pl.BlockSpec(memory_space=pltpu.VMEM)
    return pl.pallas_call(
        gather_kernel,
        out_shape=(
            jax.ShapeDtypeStruct((blocks, cells, realizations), jnp.float32),
            jax.ShapeDtypeStruct((blocks * halves, edge, LANES), jnp.float32),
        ),
        in_specs=[smem, smem, pl.BlockSpec(memory_space=pl.ANY), vmem, vmem, vmem, vmem],
        out_specs=(pl.BlockSpec(memory_space=pl.ANY), vmem),
        scratch_shapes=[
            pltpu.VMEM(pool.shape, pool.dtype),
            pltpu.VMEM((halves, entries, 2, LANES), pool.dtype),
            pltpu.VMEM((blocks, cells, realizations), jnp.float32),
            pltpu.SemaphoreType.DMA((PIECES,)),
            pltpu.SemaphoreType.DMA((blocks,)),
        ],
        compiler_params=pltpu.CompilerParams(vmem_limit_bytes=50 * 2**20),
        cost_estimate=pl.CostEstimate(
            flops=2 * blocks * cells * (2 * entries + cells) * realizations,
            bytes_accessed=5 * 2**24,
            transcendentals=0,
        ),
        name="gather",
    )(tile, count, pool, live, weight2, lower, draw)


def scan_kernel(scan_ref, face_ref, out_ref):
    out_ref[...] = jnp.dot(
        scan_ref[...], face_ref[...], precision=HIGHEST, preferred_element_type=jnp.float32
    )


def scan_call(scan, face):
    return pl.pallas_call(
        scan_kernel,
        out_shape=jax.ShapeDtypeStruct(face.shape, face.dtype),
        compiler_params=pltpu.CompilerParams(vmem_limit_bytes=16 * 2**20),
        name="scan",
    )(scan, face)


def finish_kernel(local_ref, face_ref, below_ref, out_ref):
    blocks, _, realizations = local_ref.shape
    halves = realizations // LANES
    for b in range(blocks):
        below = jnp.concatenate([below_ref[halves * b + h] for h in range(halves)], axis=1)
        state = local_ref[b] + jnp.dot(
            face_ref[...], below, precision=HIGHEST, preferred_element_type=jnp.float32
        )
        out_ref[b] = state.astype(out_ref.dtype)


def finish_call(local, face, below):
    blocks, cells, realizations = local.shape
    edge = face.shape[1]
    halves = realizations // LANES
    size = FINISH_BLOCKS
    whole = pl.BlockSpec((size, cells, realizations), lambda b: (b, 0, 0))
    return pl.pallas_call(
        finish_kernel,
        grid=(blocks // size,),
        out_shape=jax.ShapeDtypeStruct(local.shape, jnp.bfloat16),
        in_specs=[
            whole,
            pl.BlockSpec((cells, edge), lambda b: (0, 0)),
            pl.BlockSpec((size * halves, edge, LANES), lambda b: (b, 0, 0)),
        ],
        out_specs=whole,
        name="finish",
    )(local, face, below)


def scan_matrix(square, count):
    edge = square.shape[0]
    mm = functools.partial(jnp.dot, precision=HIGHEST)
    powers = jnp.concatenate([square, jnp.eye(edge, dtype=square.dtype)], axis=1)
    top = mm(square, square)
    while powers.shape[1] < count * edge:
        powers = jnp.concatenate([mm(top, powers), powers], axis=1)
        top = mm(top, top)
    powers = powers[:, -(count - 1) * edge :]
    strip = jnp.concatenate([powers, jnp.zeros((edge, count * edge), powers.dtype)], axis=1)
    starts = [(count - 1 - f) * edge for f in range(count)]
    return jnp.concatenate([strip[:, s : s + count * edge] for s in starts])


def body(
    pool, nbr_owner, nbr_row, nbr_count, normal_draw, kriging_weight, noise_factor, face_weight
):
    pool_rows, realizations = pool.shape[1:]
    entries = nbr_row.shape[2]
    edge = face_weight.shape[1]
    halves = realizations // LANES
    front_count = lax.axis_size("front")
    group = 2 * PAIRS
    gathered = lax.all_gather(pool[0], "tile", tiled=True)
    pieces = gathered.reshape(-1, PAIRS, 2, halves, LANES).transpose(0, 3, 1, 2, 4)
    pieces = pieces.reshape(-1, 2, LANES)
    index = nbr_owner[0, :, :, 0] * pool_rows + nbr_row[0]
    tile = index // group * (halves * PAIRS) + index % group // 2
    count = nbr_count[0]
    is_live = jnp.arange(entries)[None, :] < count[:, None]
    live = (index & 1)[:, :, None] == jnp.arange(2)[None, None, :]
    live = (live & is_live[:, :, None]).astype(jnp.bfloat16).reshape(-1, 1, 2 * entries)
    weight2 = jnp.repeat(kriging_weight, 2, axis=1)
    scan = scan_matrix(face_weight[-edge:], front_count)
    local, face = gather_call(
        tile.reshape(-1), count, pieces, live, weight2, jnp.tril(noise_factor), normal_draw[0], edge
    )
    swap = functools.partial(
        lax.all_to_all, axis_name="front", split_axis=0, concat_axis=0, tiled=True
    )
    below = scan_call(scan, swap(face).reshape(-1, LANES)).reshape(face.shape)
    return finish_call(local, face_weight, swap(below))[None]


def solution(mesh):
    placed = (
        P("front", "tile", None),
        P("front", "tile", None, None),
        P("front", "tile", None),
        P("front", "tile"),
        P("front", "tile", None, None),
        P(),
        P(),
        P(),
    )
    return jax.shard_map(
        body, mesh=mesh, in_specs=placed, out_specs=P("front", "tile", None, None), check_vma=False
    )
```

```python
import functools

import jax
import jax.numpy as jnp
from jax import lax
from jax.experimental import pallas as pl
from jax.experimental.pallas import tpu as pltpu
from jax.sharding import PartitionSpec as P

LANES = 128
UNROLL = 32
PIECES = 16
PAIRS = 4
HIGHEST = lax.Precision.HIGHEST


def gather_kernel(
    tile_ref, count_ref, pool_hbm, live_ref, weight_ref, noise_ref, draw_ref,
    local_ref, edge_ref, pool, values, sems,
):
    blocks, cells, _ = local_ref.shape
    halves, entries = values.shape[:2]
    edge = edge_ref.shape[1]
    rows = pool.shape[0] // PIECES
    copies = [
        pltpu.make_async_copy(
            pool_hbm.at[pl.ds(i * rows, rows)], pool.at[pl.ds(i * rows, rows)], sems.at[i]
        )
        for i in range(PIECES)
    ]
    for copy in copies:
        copy.start()
    values[...] = jnp.zeros_like(values)
    for b in range(blocks):
        local_ref[b] = jnp.dot(
            noise_ref[...], draw_ref[b], preferred_element_type=jnp.float32
        )
    for copy in copies:
        copy.wait()

    def block(b, _):
        def some(i, _):
            base = pl.multiple_of(i * UNROLL, UNROLL)
            places = [tile_ref[b * entries + base + u] for u in range(UNROLL)]
            found = [[pool[p + h * PAIRS] for p in places] for h in range(halves)]
            for h in range(halves):
                for u in range(UNROLL):
                    values[h, base + u] = found[h][u]
            return 0

        lax.fori_loop(0, (count_ref[b] + UNROLL - 1) // UNROLL, some, 0)
        listed = jnp.concatenate(
            [values.at[h].reshape(2 * entries, LANES)[...] for h in range(halves)], axis=1
        )
        total = local_ref[b] + jnp.dot(
            weight_ref[...] * live_ref[b], listed, preferred_element_type=jnp.float32
        )
        local_ref[b] = total
        for h in range(halves):
            edge_ref[halves * b + h] = total[cells - edge :, h * LANES : (h + 1) * LANES]
        return 0

    lax.fori_loop(0, blocks, block, 0)


def gather_call(tile, count, pool, live, weight2, lower, draw, edge):
    blocks, cells, realizations = draw.shape
    halves = realizations // LANES
    entries = tile.shape[0] // blocks
    smem = pl.BlockSpec(memory_space=pltpu.SMEM)
    vmem = pl.BlockSpec(memory_space=pltpu.VMEM)
    return pl.pallas_call(
        gather_kernel,
        out_shape=(
            jax.ShapeDtypeStruct((blocks, cells, realizations), jnp.float32),
            jax.ShapeDtypeStruct((blocks * halves, edge, LANES), jnp.float32),
        ),
        in_specs=[smem, smem, pl.BlockSpec(memory_space=pltpu.HBM), vmem, vmem, vmem, vmem],
        out_specs=(vmem, vmem),
        scratch_shapes=[
            pltpu.VMEM(pool.shape, pool.dtype),
            pltpu.VMEM((halves, entries, 2, LANES), pool.dtype),
            pltpu.SemaphoreType.DMA((PIECES,)),
        ],
        compiler_params=pltpu.CompilerParams(vmem_limit_bytes=46 * 2**20),
        cost_estimate=pl.CostEstimate(
            flops=2 * blocks * cells * (2 * entries + cells) * realizations,
            bytes_accessed=5 * 2**24,
            transcendentals=0,
        ),
        name="gather",
    )(tile, count, pool, live, weight2, lower, draw)


def scan_kernel(scan_ref, face_ref, out_ref):
    out_ref[...] = jnp.dot(
        scan_ref[...], face_ref[...], precision=HIGHEST, preferred_element_type=jnp.float32
    )


def scan_call(scan, face):
    return pl.pallas_call(
        scan_kernel,
        out_shape=jax.ShapeDtypeStruct(face.shape, face.dtype),
        compiler_params=pltpu.CompilerParams(vmem_limit_bytes=16 * 2**20),
        name="scan",
    )(scan, face)


def finish_kernel(local_ref, face_ref, below_ref, out_ref):
    blocks, _, realizations = local_ref.shape
    halves = realizations // LANES
    for b in range(blocks):
        below = jnp.concatenate([below_ref[halves * b + h] for h in range(halves)], axis=1)
        state = local_ref[b] + jnp.dot(
            face_ref[...], below, precision=HIGHEST, preferred_element_type=jnp.float32
        )
        out_ref[b] = state.astype(out_ref.dtype)


def finish_call(local, face, below):
    return pl.pallas_call(
        finish_kernel,
        out_shape=jax.ShapeDtypeStruct(local.shape, jnp.bfloat16),
        compiler_params=pltpu.CompilerParams(vmem_limit_bytes=12 * 2**20),
        name="finish",
    )(local, face, below)


def scan_matrix(square, count):
    edge = square.shape[0]
    mm = functools.partial(jnp.dot, precision=HIGHEST)
    powers = jnp.concatenate([square, jnp.eye(edge, dtype=square.dtype)], axis=1)
    top = mm(square, square)
    while powers.shape[1] < count * edge:
        powers = jnp.concatenate([mm(top, powers), powers], axis=1)
        top = mm(top, top)
    powers = powers[:, -(count - 1) * edge :]
    strip = jnp.concatenate([powers, jnp.zeros((edge, count * edge), powers.dtype)], axis=1)
    starts = [(count - 1 - f) * edge for f in range(count)]
    return jnp.concatenate([strip[:, s : s + count * edge] for s in starts])


def body(
    pool, nbr_owner, nbr_row, nbr_count, normal_draw, kriging_weight, noise_factor, face_weight
):
    pool_rows, realizations = pool.shape[1:]
    entries = nbr_row.shape[2]
    edge = face_weight.shape[1]
    halves = realizations // LANES
    front_count = lax.axis_size("front")
    group = 2 * PAIRS
    gathered = lax.all_gather(pool[0], "tile", tiled=True)
    pieces = gathered.reshape(-1, PAIRS, 2, halves, LANES).transpose(0, 3, 1, 2, 4)
    pieces = pieces.reshape(-1, 2, LANES)
    index = nbr_owner[0, :, :, 0] * pool_rows + nbr_row[0]
    tile = index // group * (halves * PAIRS) + index % group // 2
    count = nbr_count[0]
    is_live = jnp.arange(entries)[None, :] < count[:, None]
    live = (index & 1)[:, :, None] == jnp.arange(2)[None, None, :]
    live = (live & is_live[:, :, None]).astype(jnp.bfloat16).reshape(-1, 1, 2 * entries)
    weight2 = jnp.repeat(kriging_weight, 2, axis=1)
    scan = scan_matrix(face_weight[-edge:], front_count)
    local, face = gather_call(
        tile.reshape(-1), count, pieces, live, weight2, jnp.tril(noise_factor), normal_draw[0], edge
    )
    swap = functools.partial(
        lax.all_to_all, axis_name="front", split_axis=0, concat_axis=0, tiled=True
    )
    below = scan_call(scan, swap(face).reshape(-1, LANES)).reshape(face.shape)
    return finish_call(local, face_weight, swap(below))[None]


def solution(mesh):
    placed = (
        P("front", "tile", None),
        P("front", "tile", None, None),
        P("front", "tile", None),
        P("front", "tile"),
        P("front", "tile", None, None),
        P(),
        P(),
        P(),
    )
    return jax.shard_map(
        body, mesh=mesh, in_specs=placed, out_specs=P("front", "tile", None, None), check_vma=False
    )
```

```python
import functools

import jax
import jax.numpy as jnp
from jax import lax
from jax.experimental import pallas as pl
from jax.experimental.pallas import tpu as pltpu
from jax.sharding import PartitionSpec as P

LANES = 128
UNROLL = 32
PIECES = 16
PAIRS = 4
HIGHEST = lax.Precision.HIGHEST


def gather_kernel(
    tile_ref, count_ref, pool_hbm, live_ref, weight_ref, noise_ref, draw_ref,
    local_ref, edge_ref, pool, values, sems,
):
    blocks, cells, _ = local_ref.shape
    halves, entries = values.shape[:2]
    edge = edge_ref.shape[1]
    rows = pool.shape[0] // PIECES
    copies = [
        pltpu.make_async_copy(
            pool_hbm.at[pl.ds(i * rows, rows)], pool.at[pl.ds(i * rows, rows)], sems.at[i]
        )
        for i in range(PIECES)
    ]
    for copy in copies:
        copy.start()
    values[...] = jnp.zeros_like(values)
    for b in range(blocks):
        local_ref[b] = jnp.dot(
            noise_ref[...], draw_ref[b], preferred_element_type=jnp.float32
        )
    for copy in copies:
        copy.wait()

    def block(b, _):
        def some(i, _):
            base = pl.multiple_of(i * UNROLL, UNROLL)
            places = [tile_ref[b * entries + base + u] for u in range(UNROLL)]
            found = [[pool[p + h * PAIRS] for p in places] for h in range(halves)]
            for h in range(halves):
                for u in range(UNROLL):
                    values[h, base + u] = found[h][u]
            return 0

        lax.fori_loop(0, (count_ref[b] + UNROLL - 1) // UNROLL, some, 0)
        listed = jnp.concatenate(
            [values.at[h].reshape(2 * entries, LANES)[...] for h in range(halves)], axis=1
        )
        total = local_ref[b] + jnp.dot(
            weight_ref[...] * live_ref[b], listed, preferred_element_type=jnp.float32
        )
        local_ref[b] = total
        for h in range(halves):
            edge_ref[halves * b + h] = total[cells - edge :, h * LANES : (h + 1) * LANES]
        return 0

    lax.fori_loop(0, blocks, block, 0)


def gather_call(tile, count, pool, live, weight2, lower, draw, edge):
    blocks, cells, realizations = draw.shape
    halves = realizations // LANES
    entries = tile.shape[0] // blocks
    smem = pl.BlockSpec(memory_space=pltpu.SMEM)
    vmem = pl.BlockSpec(memory_space=pltpu.VMEM)
    return pl.pallas_call(
        gather_kernel,
        out_shape=(
            jax.ShapeDtypeStruct((blocks, cells, realizations), jnp.float32),
            jax.ShapeDtypeStruct((blocks * halves, edge, LANES), jnp.float32),
        ),
        in_specs=[smem, smem, pl.BlockSpec(memory_space=pltpu.HBM), vmem, vmem, vmem, vmem],
        out_specs=(vmem, vmem),
        scratch_shapes=[
            pltpu.VMEM(pool.shape, pool.dtype),
            pltpu.VMEM((halves, entries, 2, LANES), pool.dtype),
            pltpu.SemaphoreType.DMA((PIECES,)),
        ],
        compiler_params=pltpu.CompilerParams(vmem_limit_bytes=46 * 2**20),
        cost_estimate=pl.CostEstimate(
            flops=2 * blocks * cells * (2 * entries + cells) * realizations,
            bytes_accessed=5 * 2**24,
            transcendentals=0,
        ),
        name="gather",
    )(tile, count, pool, live, weight2, lower, draw)


def scan_kernel(near_ref, far_ref, face_ref, out_ref):
    mm = functools.partial(jnp.dot, precision=HIGHEST, preferred_element_type=jnp.float32)
    half = near_ref.shape[0]
    low, high = face_ref[:half], face_ref[half:]
    out_ref[:half] = mm(near_ref[...], low)
    out_ref[half:] = mm(far_ref[...], low) + mm(near_ref[...], high)


def scan_call(near, far, face):
    return pl.pallas_call(
        scan_kernel,
        out_shape=jax.ShapeDtypeStruct(face.shape, face.dtype),
        compiler_params=pltpu.CompilerParams(vmem_limit_bytes=12 * 2**20),
        name="scan",
    )(near, far, face)


def finish_kernel(local_ref, face_ref, below_ref, out_hbm, done, sems):
    blocks, _, realizations = local_ref.shape
    halves = realizations // LANES
    copies = [pltpu.make_async_copy(done.at[b], out_hbm.at[b], sems.at[b]) for b in range(blocks)]
    for b in range(blocks):
        below = jnp.concatenate([below_ref[halves * b + h] for h in range(halves)], axis=1)
        state = local_ref[b] + jnp.dot(
            face_ref[...], below, precision=HIGHEST, preferred_element_type=jnp.float32
        )
        done[b] = state.astype(done.dtype)
        copies[b].start()
    for copy in copies:
        copy.wait()


def finish_call(local, face, below):
    vmem = pl.BlockSpec(memory_space=pltpu.VMEM)
    return pl.pallas_call(
        finish_kernel,
        out_shape=jax.ShapeDtypeStruct(local.shape, jnp.bfloat16),
        in_specs=[vmem, vmem, vmem],
        out_specs=pl.BlockSpec(memory_space=pl.ANY),
        scratch_shapes=[
            pltpu.VMEM(local.shape, jnp.bfloat16),
            pltpu.SemaphoreType.DMA((local.shape[0],)),
        ],
        compiler_params=pltpu.CompilerParams(vmem_limit_bytes=12 * 2**20),
        name="finish",
    )(local, face, below)


def scan_matrices(square, count):
    edge = square.shape[0]
    half = count // 2
    mm = functools.partial(jnp.dot, precision=HIGHEST)
    powers = jnp.concatenate([square, jnp.eye(edge, dtype=square.dtype)], axis=1)
    top = mm(square, square)
    while powers.shape[1] < count * edge:
        powers = jnp.concatenate([mm(top, powers), powers], axis=1)
        top = mm(top, top)
    powers = powers[:, -(count - 1) * edge :]
    strip = jnp.concatenate([powers, jnp.zeros((edge, half * edge), powers.dtype)], axis=1)

    def rows(first):
        starts = [(count - 1 - first - f) * edge for f in range(half)]
        return jnp.concatenate([strip[:, s : s + half * edge] for s in starts])

    return rows(0), rows(half)


def body(
    pool, nbr_owner, nbr_row, nbr_count, normal_draw, kriging_weight, noise_factor, face_weight
):
    pool_rows, realizations = pool.shape[1:]
    entries = nbr_row.shape[2]
    edge = face_weight.shape[1]
    halves = realizations // LANES
    front_count = lax.axis_size("front")
    group = 2 * PAIRS
    gathered = lax.all_gather(pool[0], "tile", tiled=True)
    pieces = gathered.reshape(-1, PAIRS, 2, halves, LANES).transpose(0, 3, 1, 2, 4)
    pieces = pieces.reshape(-1, 2, LANES)
    index = nbr_owner[0, :, :, 0] * pool_rows + nbr_row[0]
    tile = index // group * (halves * PAIRS) + index % group // 2
    count = nbr_count[0]
    is_live = jnp.arange(entries)[None, :] < count[:, None]
    live = (index & 1)[:, :, None] == jnp.arange(2)[None, None, :]
    live = (live & is_live[:, :, None]).astype(jnp.bfloat16).reshape(-1, 1, 2 * entries)
    weight2 = jnp.repeat(kriging_weight, 2, axis=1)
    near, far = scan_matrices(face_weight[-edge:], front_count)
    local, face = gather_call(
        tile.reshape(-1), count, pieces, live, weight2, jnp.tril(noise_factor), normal_draw[0], edge
    )
    swap = functools.partial(
        lax.all_to_all, axis_name="front", split_axis=0, concat_axis=0, tiled=True
    )
    below = scan_call(near, far, swap(face).reshape(-1, LANES)).reshape(face.shape)
    return finish_call(local, face_weight, swap(below))[None]


def solution(mesh):
    placed = (
        P("front", "tile", None),
        P("front", "tile", None, None),
        P("front", "tile", None),
        P("front", "tile"),
        P("front", "tile", None, None),
        P(),
        P(),
        P(),
    )
    return jax.shard_map(
        body, mesh=mesh, in_specs=placed, out_specs=P("front", "tile", None, None), check_vma=False
    )
```

```python
import functools

import jax
import jax.numpy as jnp
from jax import lax
from jax.experimental import pallas as pl
from jax.experimental.pallas import tpu as pltpu
from jax.sharding import PartitionSpec as P

LANES = 128
UNROLL = 32
PIECES = 16
PAIRS = 4
HIGHEST = lax.Precision.HIGHEST


def gather_kernel(
    tile_ref, count_ref, pool_hbm, live_ref, weight_ref, noise_ref, draw_ref,
    local_ref, edge_ref, pool, values, sems,
):
    blocks, cells, _ = local_ref.shape
    halves, entries = values.shape[:2]
    edge = edge_ref.shape[1]
    rows = pool.shape[0] // PIECES
    copies = [
        pltpu.make_async_copy(
            pool_hbm.at[pl.ds(i * rows, rows)], pool.at[pl.ds(i * rows, rows)], sems.at[i]
        )
        for i in range(PIECES)
    ]
    for copy in copies:
        copy.start()
    values[...] = jnp.zeros_like(values)
    for b in range(blocks):
        local_ref[b] = jnp.dot(
            noise_ref[...], draw_ref[b], preferred_element_type=jnp.float32
        )
    for copy in copies:
        copy.wait()

    def block(b, _):
        def some(i, _):
            base = pl.multiple_of(i * UNROLL, UNROLL)
            places = [tile_ref[b * entries + base + u] for u in range(UNROLL)]
            found = [[pool[p + h * PAIRS] for p in places] for h in range(halves)]
            for h in range(halves):
                for u in range(UNROLL):
                    values[h, base + u] = found[h][u]
            return 0

        lax.fori_loop(0, (count_ref[b] + UNROLL - 1) // UNROLL, some, 0)
        listed = jnp.concatenate(
            [values.at[h].reshape(2 * entries, LANES)[...] for h in range(halves)], axis=1
        )
        total = local_ref[b] + jnp.dot(
            weight_ref[...] * live_ref[b], listed, preferred_element_type=jnp.float32
        )
        local_ref[b] = total
        for h in range(halves):
            edge_ref[halves * b + h] = total[cells - edge :, h * LANES : (h + 1) * LANES]
        return 0

    lax.fori_loop(0, blocks, block, 0)


def gather_call(tile, count, pool, live, weight2, lower, draw, edge):
    blocks, cells, realizations = draw.shape
    halves = realizations // LANES
    entries = tile.shape[0] // blocks
    smem = pl.BlockSpec(memory_space=pltpu.SMEM)
    vmem = pl.BlockSpec(memory_space=pltpu.VMEM)
    return pl.pallas_call(
        gather_kernel,
        out_shape=(
            jax.ShapeDtypeStruct((blocks, cells, realizations), jnp.float32),
            jax.ShapeDtypeStruct((blocks * halves, edge, LANES), jnp.float32),
        ),
        in_specs=[smem, smem, pl.BlockSpec(memory_space=pltpu.HBM), vmem, vmem, vmem, vmem],
        out_specs=(vmem, vmem),
        scratch_shapes=[
            pltpu.VMEM(pool.shape, pool.dtype),
            pltpu.VMEM((halves, entries, 2, LANES), pool.dtype),
            pltpu.SemaphoreType.DMA((PIECES,)),
        ],
        compiler_params=pltpu.CompilerParams(vmem_limit_bytes=46 * 2**20),
        cost_estimate=pl.CostEstimate(
            flops=2 * blocks * cells * (2 * entries + cells) * realizations,
            bytes_accessed=5 * 2**24,
            transcendentals=0,
        ),
        name="gather",
    )(tile, count, pool, live, weight2, lower, draw)


def scan_kernel(strip_ref, face_ref, out_ref, near, far):
    mm = functools.partial(jnp.dot, precision=HIGHEST, preferred_element_type=jnp.float32)
    edge, half = strip_ref.shape[0], near.shape[0]
    fronts = 2 * half // edge
    for f in range(fronts // 2):
        for matrix, first in ((near, 0), (far, fronts // 2)):
            start = (fronts - 1 - first - f) * edge
            matrix[f * edge : (f + 1) * edge, :] = strip_ref[:, start : start + half]
    low, high = face_ref[:half], face_ref[half:]
    out_ref[:half] = mm(near[...], low)
    out_ref[half:] = mm(far[...], low) + mm(near[...], high)


def scan_call(strip, face):
    half = face.shape[0] // 2
    return pl.pallas_call(
        scan_kernel,
        out_shape=jax.ShapeDtypeStruct(face.shape, face.dtype),
        scratch_shapes=[pltpu.VMEM((half, half), face.dtype)] * 2,
        compiler_params=pltpu.CompilerParams(vmem_limit_bytes=12 * 2**20),
        name="scan",
    )(strip, face)


def finish_kernel(local_ref, face_ref, below_ref, out_hbm, done, sems):
    blocks, _, realizations = local_ref.shape
    halves = realizations // LANES
    copies = [pltpu.make_async_copy(done.at[b], out_hbm.at[b], sems.at[b]) for b in range(blocks)]
    for b in range(blocks):
        below = jnp.concatenate([below_ref[halves * b + h] for h in range(halves)], axis=1)
        state = local_ref[b] + jnp.dot(
            face_ref[...], below, precision=HIGHEST, preferred_element_type=jnp.float32
        )
        done[b] = state.astype(done.dtype)
        copies[b].start()
    for copy in copies:
        copy.wait()


def finish_call(local, face, below):
    vmem = pl.BlockSpec(memory_space=pltpu.VMEM)
    return pl.pallas_call(
        finish_kernel,
        out_shape=jax.ShapeDtypeStruct(local.shape, jnp.bfloat16),
        in_specs=[vmem, vmem, vmem],
        out_specs=pl.BlockSpec(memory_space=pl.ANY),
        scratch_shapes=[
            pltpu.VMEM(local.shape, jnp.bfloat16),
            pltpu.SemaphoreType.DMA((local.shape[0],)),
        ],
        compiler_params=pltpu.CompilerParams(vmem_limit_bytes=12 * 2**20),
        name="finish",
    )(local, face, below)


def scan_strip(square, count):
    edge = square.shape[0]
    mm = functools.partial(jnp.dot, precision=HIGHEST)
    powers = jnp.concatenate([square, jnp.eye(edge, dtype=square.dtype)], axis=1)
    top = mm(square, square)
    while powers.shape[1] < count * edge:
        powers = jnp.concatenate([mm(top, powers), powers], axis=1)
        top = mm(top, top)
    powers = powers[:, -(count - 1) * edge :]
    zeros = jnp.zeros((edge, count // 2 * edge), powers.dtype)
    return jnp.concatenate([powers, zeros], axis=1)


def body(
    pool, nbr_owner, nbr_row, nbr_count, normal_draw, kriging_weight, noise_factor, face_weight
):
    pool_rows, realizations = pool.shape[1:]
    entries = nbr_row.shape[2]
    edge = face_weight.shape[1]
    halves = realizations // LANES
    front_count = lax.axis_size("front")
    group = 2 * PAIRS
    gathered = lax.all_gather(pool[0], "tile", tiled=True)
    pieces = gathered.reshape(-1, PAIRS, 2, halves, LANES).transpose(0, 3, 1, 2, 4)
    pieces = pieces.reshape(-1, 2, LANES)
    index = nbr_owner[0, :, :, 0] * pool_rows + nbr_row[0]
    tile = index // group * (halves * PAIRS) + index % group // 2
    count = nbr_count[0]
    is_live = jnp.arange(entries)[None, :] < count[:, None]
    live = (index & 1)[:, :, None] == jnp.arange(2)[None, None, :]
    live = (live & is_live[:, :, None]).astype(jnp.bfloat16).reshape(-1, 1, 2 * entries)
    weight2 = jnp.repeat(kriging_weight, 2, axis=1)
    strip = scan_strip(face_weight[-edge:], front_count)
    local, face = gather_call(
        tile.reshape(-1), count, pieces, live, weight2, jnp.tril(noise_factor), normal_draw[0], edge
    )
    swap = functools.partial(
        lax.all_to_all, axis_name="front", split_axis=0, concat_axis=0, tiled=True
    )
    below = scan_call(strip, swap(face).reshape(-1, LANES)).reshape(face.shape)
    return finish_call(local, face_weight, swap(below))[None]


def solution(mesh):
    placed = (
        P("front", "tile", None),
        P("front", "tile", None, None),
        P("front", "tile", None),
        P("front", "tile"),
        P("front", "tile", None, None),
        P(),
        P(),
        P(),
    )
    return jax.shard_map(
        body, mesh=mesh, in_specs=placed, out_specs=P("front", "tile", None, None), check_vma=False
    )
```

```python
import functools

import jax
import jax.numpy as jnp
from jax import lax
from jax.experimental import pallas as pl
from jax.experimental.pallas import tpu as pltpu
from jax.sharding import PartitionSpec as P

LANES = 128
UNROLL = 32
PIECES = 16
PAIRS = 4
HIGHEST = lax.Precision.HIGHEST


def gather_kernel(
    tile_ref, count_ref, pool_hbm, live_ref, weight_ref, noise_ref, draw_ref, strip_ref,
    local_ref, edge_ref, pool, values, sems,
):
    blocks, cells, _ = local_ref.shape
    halves, entries = values.shape[:2]
    edge = edge_ref.shape[1]
    rows = pool.shape[0] // PIECES
    copies = [
        pltpu.make_async_copy(
            pool_hbm.at[pl.ds(i * rows, rows)], pool.at[pl.ds(i * rows, rows)], sems.at[i]
        )
        for i in range(PIECES)
    ]
    for copy in copies:
        copy.start()
    values[...] = jnp.zeros_like(values)
    for b in range(blocks):
        local_ref[b] = jnp.dot(
            noise_ref[...], draw_ref[b], preferred_element_type=jnp.float32
        )
    for copy in copies:
        copy.wait()

    def block(b, _):
        def some(i, _):
            base = pl.multiple_of(i * UNROLL, UNROLL)
            places = [tile_ref[b * entries + base + u] for u in range(UNROLL)]
            found = [[pool[p + h * PAIRS] for p in places] for h in range(halves)]
            for h in range(halves):
                for u in range(UNROLL):
                    values[h, base + u] = found[h][u]
            return 0

        lax.fori_loop(0, (count_ref[b] + UNROLL - 1) // UNROLL, some, 0)
        listed = jnp.concatenate(
            [values.at[h].reshape(2 * entries, LANES)[...] for h in range(halves)], axis=1
        )
        total = local_ref[b] + jnp.dot(
            weight_ref[...] * live_ref[b], listed, preferred_element_type=jnp.float32
        )
        local_ref[b] = total
        for h in range(halves):
            edge_ref[halves * b + h] = total[cells - edge :, h * LANES : (h + 1) * LANES]
        return 0

    lax.fori_loop(0, blocks, block, 0)


def gather_call(tile, count, pool, live, weight2, lower, draw, strip):
    blocks, cells, realizations = draw.shape
    halves = realizations // LANES
    edge = strip.shape[0]
    entries = tile.shape[0] // blocks
    smem = pl.BlockSpec(memory_space=pltpu.SMEM)
    vmem = pl.BlockSpec(memory_space=pltpu.VMEM)
    hbm = pl.BlockSpec(memory_space=pl.ANY)
    return pl.pallas_call(
        gather_kernel,
        out_shape=(
            jax.ShapeDtypeStruct((blocks, cells, realizations), jnp.float32),
            jax.ShapeDtypeStruct((blocks * halves, edge, LANES), jnp.float32),
        ),
        in_specs=[smem, smem, pl.BlockSpec(memory_space=pltpu.HBM), vmem, vmem, vmem, vmem, hbm],
        out_specs=(vmem, vmem),
        scratch_shapes=[
            pltpu.VMEM(pool.shape, pool.dtype),
            pltpu.VMEM((halves, entries, 2, LANES), pool.dtype),
            pltpu.SemaphoreType.DMA((PIECES,)),
        ],
        compiler_params=pltpu.CompilerParams(vmem_limit_bytes=46 * 2**20),
        cost_estimate=pl.CostEstimate(
            flops=2 * blocks * cells * (2 * entries + cells) * realizations,
            bytes_accessed=5 * 2**24,
            transcendentals=0,
        ),
        name="gather",
    )(tile, count, pool, live, weight2, lower, draw, strip)


def scan_kernel(strip_ref, face_ref, out_ref, near, far):
    mm = functools.partial(jnp.dot, precision=HIGHEST, preferred_element_type=jnp.float32)
    edge, half = strip_ref.shape[0], near.shape[0]
    fronts = 2 * half // edge
    for f in range(fronts // 2):
        for matrix, first in ((near, 0), (far, fronts // 2)):
            start = (fronts - 1 - first - f) * edge
            matrix[f * edge : (f + 1) * edge, :] = strip_ref[:, start : start + half]
    low, high = face_ref[:half], face_ref[half:]
    out_ref[:half] = mm(near[...], low)
    out_ref[half:] = mm(far[...], low) + mm(near[...], high)


def scan_call(strip, face):
    half = face.shape[0] // 2
    return pl.pallas_call(
        scan_kernel,
        out_shape=jax.ShapeDtypeStruct(face.shape, face.dtype),
        scratch_shapes=[pltpu.VMEM((half, half), face.dtype)] * 2,
        compiler_params=pltpu.CompilerParams(vmem_limit_bytes=12 * 2**20),
        name="scan",
    )(strip, face)


def finish_kernel(local_ref, face_ref, below_ref, out_hbm, done, sems):
    blocks, _, realizations = local_ref.shape
    halves = realizations // LANES
    copies = [pltpu.make_async_copy(done.at[b], out_hbm.at[b], sems.at[b]) for b in range(blocks)]
    for b in range(blocks):
        below = jnp.concatenate([below_ref[halves * b + h] for h in range(halves)], axis=1)
        state = local_ref[b] + jnp.dot(
            face_ref[...], below, precision=HIGHEST, preferred_element_type=jnp.float32
        )
        done[b] = state.astype(done.dtype)
        copies[b].start()
    for copy in copies:
        copy.wait()


def finish_call(local, face, below):
    vmem = pl.BlockSpec(memory_space=pltpu.VMEM)
    return pl.pallas_call(
        finish_kernel,
        out_shape=jax.ShapeDtypeStruct(local.shape, jnp.bfloat16),
        in_specs=[vmem, vmem, vmem],
        out_specs=pl.BlockSpec(memory_space=pl.ANY),
        scratch_shapes=[
            pltpu.VMEM(local.shape, jnp.bfloat16),
            pltpu.SemaphoreType.DMA((local.shape[0],)),
        ],
        compiler_params=pltpu.CompilerParams(vmem_limit_bytes=12 * 2**20),
        name="finish",
    )(local, face, below)


def scan_strip(square, count):
    edge = square.shape[0]
    mm = functools.partial(jnp.dot, precision=HIGHEST)
    powers = jnp.concatenate([square, jnp.eye(edge, dtype=square.dtype)], axis=1)
    top = mm(square, square)
    while powers.shape[1] < count * edge:
        powers = jnp.concatenate([mm(top, powers), powers], axis=1)
        top = mm(top, top)
    powers = powers[:, -(count - 1) * edge :]
    zeros = jnp.zeros((edge, count // 2 * edge), powers.dtype)
    return jnp.concatenate([powers, zeros], axis=1)


def body(
    pool, nbr_owner, nbr_row, nbr_count, normal_draw, kriging_weight, noise_factor, face_weight
):
    pool_rows, realizations = pool.shape[1:]
    entries = nbr_row.shape[2]
    edge = face_weight.shape[1]
    halves = realizations // LANES
    front_count = lax.axis_size("front")
    group = 2 * PAIRS
    gathered = lax.all_gather(pool[0], "tile", tiled=True)
    pieces = gathered.reshape(-1, PAIRS, 2, halves, LANES).transpose(0, 3, 1, 2, 4)
    pieces = pieces.reshape(-1, 2, LANES)
    index = nbr_owner[0, :, :, 0] * pool_rows + nbr_row[0]
    tile = index // group * (halves * PAIRS) + index % group // 2
    count = nbr_count[0]
    is_live = jnp.arange(entries)[None, :] < count[:, None]
    live = (index & 1)[:, :, None] == jnp.arange(2)[None, None, :]
    live = (live & is_live[:, :, None]).astype(jnp.bfloat16).reshape(-1, 1, 2 * entries)
    weight2 = jnp.repeat(kriging_weight, 2, axis=1)
    strip = scan_strip(face_weight[-edge:], front_count)
    local, face = gather_call(
        tile.reshape(-1), count, pieces, live, weight2, jnp.tril(noise_factor), normal_draw[0], strip
    )
    swap = functools.partial(
        lax.all_to_all, axis_name="front", split_axis=0, concat_axis=0, tiled=True
    )
    below = scan_call(strip, swap(face).reshape(-1, LANES)).reshape(face.shape)
    return finish_call(local, face_weight, swap(below))[None]


def solution(mesh):
    placed = (
        P("front", "tile", None),
        P("front", "tile", None, None),
        P("front", "tile", None),
        P("front", "tile"),
        P("front", "tile", None, None),
        P(),
        P(),
        P(),
    )
    return jax.shard_map(
        body, mesh=mesh, in_specs=placed, out_specs=P("front", "tile", None, None), check_vma=False
    )
```
